32 devices in a mesh: groups: 2 (over y), slab: 8 (over z, x), grid: 2 (over core).
Axes of the slice: x: 2, y: 2, z: 4, core: 2. Of those that a mesh axis runs over, the one named last changes fastest.
Arguments:
- grids_a: float32 [4, 3, 32, 16, 128], P(('groups', 'grid'), None, 'slab'), parts along dimension 0, may hold values from -4 to 4, as said below
- grids_b: float32 [4, 3, 64, 8, 128], P(('groups', 'grid'), None, 'slab'), parts along dimension 0, may hold values from -4 to 4, as said below
- coeffs: int32 [4], replicated, may hold values from -2 to 2
Outputs:
- out_a: float32 [4, 3, 32, 16, 128], P(('groups', 'grid'), None, 'slab'), parts along dimension 0
- out_b: float32 [4, 3, 64, 8, 128], P(('groups', 'grid'), None, 'slab'), parts along dimension 0
- combined_a: float32 [4, 3, 32, 16, 128], P(('groups', 'grid'), None, 'slab'), parts along dimension 0
- combined_b: float32 [4, 3, 64, 8, 128], P(('groups', 'grid'), None, 'slab'), parts along dimension 0
The draws below stay inside these ranges and needn't reach their ends.
There are 2 independent parts, one for each index of `groups`. The reference program is written for one: setup_inputs(seed, part) draws one part's arguments, and reference() takes and returns one part's arrays. A program takes and returns all parts, laid end to end along the dimension named above; an argument that names none is the same for every part. Nothing has to cross between parts.
Inputs may be any that keep to these rules, and one draw needn't show every extreme that they name: `coeffs`: coefficients of grids_a[0], grids_a[1], grids_b[0], grids_b[1] in this order. `grids_a`: velocity components. `grids_b`: velocity components.
All inputs are finite; a program needn't handle non-finite values.
Results may differ from the reference program's by a relative error of at most 0.0003.
Values sent between devices are 32-bit elements; how exact they have to be, the bound alone decides.
A program may use at most 64 MiB of HBM per device.

```python
import math
import jax
import jax.numpy as jnp
from jax import lax

XA = 128
YA = 16
YB = 8
ZA = 32
ZB = 64


def signed_field(key, extent, lowest):
    sign_key = jax.random.fold_in(key, 1)
    size_key = jax.random.fold_in(key, 2)
    sign_part = (2 * jax.random.randint(sign_key, extent, 0, 2) - 1).astype(jnp.float32)
    size_part = jax.random.uniform(size_key, extent, jnp.float32, lowest, 4.0)
    return sign_part * size_part


def draw_grids_a(key, part):
    key = jax.random.fold_in(key, 11)
    return signed_field(key, (2, 3, ZA, YA, XA), 3.0)


def draw_grids_b(key, part):
    key = jax.random.fold_in(key, 23)
    return signed_field(key, (2, 3, ZB, YB, XA), 3.0)


def place_ends(array, rng, least, high):
    longest = array.shape.index(max(array.shape))
    spots = []
    for shift in (0, 1):
        where = [jax.random.randint(jax.random.fold_in(rng, axis), (), 0, length) for axis, length in enumerate(array.shape)]
        where[longest] = (where[longest] + shift) % array.shape[longest]
        spots.append(tuple(where))
    return array.at[spots[0]].set(least).at[spots[1]].set(high)


def setup_inputs(seed: int = 0, part: int = 0) -> dict:
    key_list = jax.random.split(jax.random.key(seed), 4)
    part_splits = jax.random.split(jax.random.fold_in(key_list[3], part), 4)
    grids_a = draw_grids_a(jax.random.fold_in(jax.random.fold_in(key_list[3], part), 71), part)
    grids_b = draw_grids_b(jax.random.fold_in(jax.random.fold_in(key_list[3], part), 71), part)
    coeffs = place_ends(jax.random.randint(key_list[2], (4,), -2, 3), jax.random.fold_in(key_list[2], 1), -2, 2).astype(jnp.int32)
    return dict(grids_a=grids_a, grids_b=grids_b, coeffs=coeffs)


first_coef = (0.8, -0.2, 4.0 / 105.0, -1.0 / 280.0)
second_coef = (1.6, -0.2, 8.0 / 315.0, -1.0 / 560.0)
second_mid = -205.0 / 72.0


def periodic_terms(values, dimension, spacing):
    gradient = jnp.zeros_like(values)
    curvature = second_mid * values
    for offset in range(1, 5):
        forward = jnp.roll(values, -offset, dimension)
        behind = jnp.roll(values, offset, dimension)
        gradient = gradient + first_coef[offset - 1] * (forward - behind)
        curvature = curvature + second_coef[offset - 1] * (forward + behind)
    return gradient / spacing, curvature / (spacing * spacing)


def burgers_rate(values, spacings, viscosity):
    z_grad, z_curv = periodic_terms(values, 1, spacings[0])
    y_grad, y_curv = periodic_terms(values, 2, spacings[1])
    x_grad, x_curv = periodic_terms(values, 3, spacings[2])
    carried = values[0:1] * x_grad + values[1:2] * y_grad + values[2:3] * z_grad
    return viscosity * (x_curv + y_curv + z_curv) - carried


def runge_kutta(values, tendency, time_step):
    k_one = tendency(values)
    k_two = tendency(values + 0.5 * time_step * k_one)
    k_three = tendency(values + 0.5 * time_step * k_two)
    k_four = tendency(values + time_step * k_three)
    return values + (time_step / 6.0) * (k_one + 2.0 * k_two + 2.0 * k_three + k_four)


def hier_axis(values, dimension, sense):
    leading = jnp.moveaxis(values, dimension, 0)
    length = leading.shape[0]
    strides = []
    stride = 1
    while stride < length:
        strides.append(stride)
        stride = stride * 2
    if sense > 0:
        strides = strides[::-1]
    for stride in strides:
        blocks = leading.reshape((length // (2 * stride), 2 * stride) + leading.shape[1:])
        left_node = blocks[:, 0]
        right_node = jnp.roll(left_node, -1, 0)
        middle = blocks[:, stride] + sense * 0.5 * (left_node + right_node)
        blocks = blocks.at[:, stride].set(middle)
        leading = blocks.reshape(leading.shape)
    return jnp.moveaxis(leading, 0, dimension)


def carry_over(source, target_dims):
    result = source
    for dimension in (1, 2, 3):
        have_cells = result.shape[dimension]
        want_cells = target_dims[dimension - 1]
        common = min(have_cells, want_cells)
        result = lax.slice_in_dim(result, 0, have_cells, have_cells // common, dimension)
        factor = want_cells // common
        if factor > 1:
            spread = jnp.expand_dims(result, dimension + 1)
            widths = [(0, 0)] * spread.ndim
            widths[dimension + 1] = (0, factor - 1)
            spread = jnp.pad(spread, widths)
            new_shape = list(result.shape)
            new_shape[dimension] = want_cells
            result = spread.reshape(new_shape)
    return result


def swap_frame(values):
    turned = jnp.stack([values[1], values[0], values[2]])
    return jnp.swapaxes(turned, 2, 3)


def gather_terms(target_dims, pieces):
    summed = None
    for weight, source in pieces:
        term = weight * carry_over(source, target_dims)
        summed = term if summed is None else summed + term
    return summed


def reference(grids_a, grids_b, coeffs):
    finest = 2.0 * math.pi / max(XA, 2 * ZA)
    time_step = 0.1 * finest
    viscosity = 0.2 * finest
    spacing_a = (2.0 * math.pi / ZA, 2.0 * math.pi / YA, 2.0 * math.pi / XA)
    spacing_b = (2.0 * math.pi / ZB, 2.0 * math.pi / YB, 2.0 * math.pi / XA)
    weights = coeffs.astype(jnp.float32)
    surplus_a = []
    surplus_b = []
    for member in range(2):
        moved_a = runge_kutta(grids_a[member], lambda v: burgers_rate(v, spacing_a, viscosity), time_step)
        moved_b = runge_kutta(grids_b[member], lambda v: burgers_rate(v, spacing_b, viscosity), time_step)
        for dimension in (3, 2, 1):
            moved_a = hier_axis(moved_a, dimension, -1)
            moved_b = hier_axis(moved_b, dimension, -1)
        surplus_a.append(moved_a)
        surplus_b.append(moved_b)
    outs_a = []
    outs_b = []
    sums_a = []
    sums_b = []
    for member in range(2):
        partner = 1 - member
        pieces = [(weights[member], surplus_a[member]), (weights[2 + member], surplus_b[member]),
                  (weights[partner], swap_frame(surplus_a[partner])),
                  (weights[2 + partner], swap_frame(surplus_b[partner]))]
        joined_a = gather_terms(surplus_a[member].shape[1:], pieces)
        joined_b = gather_terms(surplus_b[member].shape[1:], pieces)
        sums_a.append(joined_a)
        sums_b.append(joined_b)
        for dimension in (1, 2, 3):
            joined_a = hier_axis(joined_a, dimension, 1)
            joined_b = hier_axis(joined_b, dimension, 1)
        outs_a.append(joined_a)
        outs_b.append(joined_b)
    return (jnp.stack(outs_a), jnp.stack(outs_b), jnp.stack(sums_a), jnp.stack(sums_b))
```

```python
import functools
import math

import jax
import jax.numpy as jnp
import ml_dtypes
import numpy as np
from jax import lax
from jax.experimental import pallas as pl
from jax.experimental.pallas import tpu as pltpu
from jax.sharding import PartitionSpec as P

first_coef = (0.8, -0.2, 4.0 / 105.0, -1.0 / 280.0)
second_coef = (1.6, -0.2, 8.0 / 315.0, -1.0 / 560.0)
second_mid = -205.0 / 72.0
MESH = pl.DeviceIdType.MESH


def hier_matrix(n):
    m = np.eye(n)
    for i in range(1, n):
        s = i & -i
        m[i, i - s] -= 0.5
        m[i, (i + s) % n] -= 0.5
    return m


def tables(za, ya, zb, yb, nx):
    hx, ha, hb = hier_matrix(nx), hier_matrix(ya), hier_matrix(yb)
    dx, da, db = (np.linalg.inv(h) for h in (hx, ha, hb))
    pa, pb = 3 * za, 3 * zb
    ratio = ya // yb
    spread_y = np.zeros((ya, yb))
    spread_y[np.arange(yb) * ratio, np.arange(yb)] = 1
    even = np.zeros((pa, pb))
    swap_a = np.zeros((pa, pa))
    swap_ab = np.zeros((pa, pb))
    swap_b = np.zeros((pb, pb))
    turned = (1, 0, 2)
    for c in range(3):
        for z in range(za):
            even[c * za + z, c * zb + 2 * z] = 1
            swap_a[c * za + z, turned[c] * za + z] = 1
            swap_ab[c * za + z, turned[c] * zb + 2 * z] = 1
        for z in range(zb):
            swap_b[c * zb + z, turned[c] * zb + z] = 1
    own_a = np.concatenate([np.kron(np.eye(pa), ha), np.kron(np.eye(pa), ha[::ratio])])
    own_b = np.concatenate([np.kron(even, spread_y @ hb), np.kron(np.eye(pb), hb)])
    pick_a, pick_b = hx[:: nx // ya], hx[:: nx // yb]
    other_a = np.concatenate([np.tile(pick_a, (pa, 1)), np.tile(pick_b, (pa, 1))])
    other_b = np.concatenate([np.tile(pick_a, (pa, 1)), np.tile(pick_b, (pb, 1))])
    mask_a = np.concatenate([np.kron(swap_a, np.ones((ya, ya))), np.kron(swap_a, np.ones((yb, ya)))])
    mask_b = np.concatenate([np.kron(swap_ab, np.ones((ya, yb))), np.kron(swap_b, np.ones((yb, yb)))])
    spread_a = np.zeros((ya, nx))
    spread_a[np.arange(ya), np.arange(ya) * (nx // ya)] = 1
    spread_b = np.zeros((yb, nx))
    spread_b[np.arange(yb), np.arange(yb) * (nx // yb)] = 1
    place_a = np.tile(ha.T @ spread_a, (pa, 1))
    place_b = np.tile(hb.T @ spread_b, (pb, 1))
    back_a = np.kron(np.eye(pa), da)
    back_b = np.kron(np.eye(pb), db)
    group = (hx.T, dx.T, own_a, own_b, other_a, other_b, mask_a, mask_b, place_a, place_b, back_a, back_b)
    return [np.asarray(m, dtype=ml_dtypes.bfloat16) for m in group]


def terms(x):
    hi = x.astype(jnp.bfloat16)
    lo = (x - hi.astype(jnp.float32)).astype(jnp.bfloat16)
    return hi, lo


def dot(a, b, contract):
    return lax.dot_general(a, b, (contract, ((), ())), preferred_element_type=jnp.float32)


def right(x, m):
    return sum(dot(t, m, ((1,), (0,))) for t in terms(x))


def left(m, x):
    return sum(dot(m, t, ((1,), (0,))) for t in terms(x))


def left_t(m, x):
    return sum(dot(m, t, ((1,), (1,))) for t in terms(x))


def body(n, step, viscosity, space_a, space_b, *refs):
    (coeffs, a_ref, b_ref, hx, dx, own_a, own_b, other_a, other_b, mask_a, mask_b,
     place_a, place_b, back_a, back_b,
     out_a, out_b, comb_a, comb_b,
     pad_a, pad_b, adv_a, adv_b, got_a, got_b, head, nxt, low, high, nodal,
     send_sem, recv_sem, swap_send, swap_recv, head_send, head_recv) = refs
    za, ya, nx = a_ref.shape[2:]
    zb, yb = b_ref.shape[2:4]
    rows = 3 * za * ya
    me = lax.axis_index("slab")
    member = lax.axis_index("grid")
    partner = 1 - member
    ahead, behind = lax.rem(me + 1, n), lax.rem(me + n - 1, n)

    distances = [2**e for e in range(n.bit_length() - 1)]
    offsets = sorted({o % n for d in distances for o in (d, n - d)})
    barrier = pltpu.get_barrier_semaphore()
    for o in offsets:
        pl.semaphore_signal(barrier, inc=1, device_id={"slab": lax.rem(me + o, n)}, device_id_type=MESH)
    pl.semaphore_signal(barrier, inc=1, device_id={"grid": partner}, device_id_type=MESH)
    pad_a[0, :, 4 : 4 + za] = a_ref[0]
    pad_b[0, :, 4 : 4 + zb] = b_ref[0]
    pl.semaphore_wait(barrier, len(offsets) + 1)

    def halo(pad, depth, stage, which):
        made = []
        for side, (first, target, peer) in enumerate(((depth, 0, ahead), (4, 4 + depth, behind))):
            made.append(pltpu.make_async_remote_copy(
                src_ref=pad.at[stage, :, pl.ds(first, 4)],
                dst_ref=pad.at[stage, :, pl.ds(target, 4)],
                send_sem=send_sem.at[stage, which, side],
                recv_sem=recv_sem.at[stage, which, side],
                device_id={"slab": peer}, device_id_type=MESH))
        for copy in made:
            copy.start()
        return made

    def flat_rate(f, spaces):
        planes, y, x = f.shape[1:]
        rows_f = f.reshape(3 * planes * y, x)
        blocks = f.reshape(3 * planes, y, x)
        mid = second_mid * viscosity * sum(1.0 / (h * h) for h in spaces)

        def direction(value, axis, h):
            grad = curv = None
            length = value.shape[axis]
            for k in range(1, 5):
                fwd = pltpu.roll(value, length - k, axis)
                bwd = pltpu.roll(value, k, axis)
                g = (first_coef[k - 1] / h) * (fwd - bwd)
                c = (viscosity * second_coef[k - 1] / (h * h)) * (fwd + bwd)
                grad = g if grad is None else grad + g
                curv = c if curv is None else curv + c
            return grad.reshape(f.shape), curv.reshape(f.shape)

        xg, xc = direction(rows_f, 1, spaces[2])
        yg, yc = direction(blocks, 1, spaces[1])
        return mid * f + xc + yc - (f[0:1] * xg + f[1:2] * yg)

    def z_rate(pad, stage, depth, h):
        f = pad[stage, :, 4 : 4 + depth]
        grad = curv = None
        for k in range(1, 5):
            fwd = pad[stage, :, 4 + k : 4 + k + depth]
            bwd = pad[stage, :, 4 - k : 4 - k + depth]
            g = (first_coef[k - 1] / h) * (fwd - bwd)
            c = (viscosity * second_coef[k - 1] / (h * h)) * (fwd + bwd)
            grad = g if grad is None else grad + g
            curv = c if curv is None else curv + c
        return curv - f[2:3] * grad

    grids = ((pad_a, za, space_a, adv_a), (pad_b, zb, space_b, adv_b))
    swaps = []
    flights = [halo(pad, depth, 0, w) for w, (pad, depth, _, _) in enumerate(grids)]
    sent = list(flights)
    for stage in range(4):
        flat = [flat_rate(pad[stage, :, 4 : 4 + depth], spaces) for pad, depth, spaces, _ in grids]
        coming = []
        for w, (pad, depth, spaces, adv) in enumerate(grids):
            for copy in flights[w]:
                copy.wait_recv()
            k = flat[w] + z_rate(pad, stage, depth, spaces[0])
            base = pad[0, :, 4 : 4 + depth]
            share = step / 6.0 * (1.0, 2.0, 2.0, 1.0)[stage]
            adv[...] = (base if stage == 0 else adv[...]) + share * k
            if stage < 3:
                pad[stage + 1, :, 4 : 4 + depth] = base + (0.5, 0.5, 1.0)[stage] * step * k
                coming.append(halo(pad, depth, stage + 1, w))
            else:
                copy = pltpu.make_async_remote_copy(
                    src_ref=adv, dst_ref=(got_a, got_b)[w],
                    send_sem=swap_send.at[w], recv_sem=swap_recv.at[w],
                    device_id={"grid": partner}, device_id_type=MESH)
                copy.start()
                swaps.append(copy)
        if stage < 3:
            flights = coming
            sent.extend(coming)

    weight = [coeffs[i].astype(jnp.float32) for i in (member, partner, 2 + member, 2 + partner)]
    mine_a = weight[0] * left(own_a[...], right(adv_a[...].reshape(rows, nx), hx[...]))
    mine_b = weight[2] * left(own_b[...], right(adv_b[...].reshape(rows, nx), hx[...]))

    def other(got, pick, mask, place):
        crossed = left_t(pick[...], got[...].reshape(rows, nx)) * mask[...].astype(jnp.float32)
        return right(crossed, place[...])

    swaps[0].wait_recv()
    sum_a = mine_a + weight[1] * other(got_a, other_a, mask_a, place_a)
    swaps[1].wait_recv()
    sum_b = mine_b + weight[3] * other(got_b, other_b, mask_b, place_b)
    nodal_a = sum_a[:rows] + sum_b[:rows]
    level_a = nodal_a.reshape(3, za, ya, nx)
    part_q = sum_a[rows:].reshape(3, za, yb, nx)
    part_p = sum_b[rows:].reshape(3, zb, yb, nx)

    head[:, 0:ya] = level_a[:, 0]
    head[:, ya : ya + yb] = part_p[:, 0]
    head[:, ya + yb : ya + 2 * yb] = part_q[:, 0]

    @pl.when(me == 0)
    def _():
        low[...] = jnp.zeros_like(low)
        high[...] = jnp.zeros_like(high)

    def head_copy(target, peer, send, recv):
        return pltpu.make_async_remote_copy(
            src_ref=head, dst_ref=target, send_sem=head_send.at[send], recv_sem=head_recv.at[recv],
            device_id={"slab": peer}, device_id_type=MESH)

    to_behind = head_copy(nxt, behind, 0, 0)
    to_behind.start()
    for e, d in enumerate(distances):
        @pl.when(lax.rem(me, 2 * d) == 0)
        def _(e=e, d=d):
            head_copy(low, lax.rem(me + d, n), 1 + 2 * e, 1).start()
            head_copy(high, lax.rem(me + n - d, n), 2 + 2 * e, 2).start()

    out_a[0] = left(back_a[...], right(nodal_a, dx[...])).reshape(3, za, ya, nx)

    to_behind.wait_recv()
    next_a = nxt[:, 0:ya]
    next_p = nxt[:, ya : ya + yb]
    next_q = nxt[:, ya + yb : ya + 2 * yb]
    for z in range(za):
        q_now = part_q[:, z]
        q_next = part_q[:, z + 1] if z + 1 < za else next_q
        p_next = part_p[:, 2 * z + 2] if z + 1 < za else next_p
        nodal[:, 2 * z] = part_p[:, 2 * z] + q_now
        nodal[:, 2 * z + 1] = part_p[:, 2 * z + 1] + 0.5 * (q_now + q_next)
        comb_b[0, :, 2 * z + 1] = part_p[:, 2 * z + 1] - 0.5 * (part_p[:, 2 * z] + p_next)
    out_b[0] = left(back_b[...], right(nodal[...].reshape(rows, nx), dx[...])).reshape(3, zb, yb, nx)

    even_b = [part_p[:, 2 * z] + part_q[:, z] for z in range(za)] + [next_p + next_q]
    even_a = [level_a[:, z] for z in range(za)] + [next_a]
    for z in range(1, za):
        s = z & -z
        comb_a[0, :, z] = even_a[z] - 0.5 * (even_a[z - s] + even_a[z + s])
        comb_b[0, :, 2 * z] = even_b[z] - 0.5 * (even_b[z - s] + even_b[z + s])

    @pl.when(me != 0)
    def _():
        head_copy(low, behind, 0, 1).wait_recv()
        head_copy(high, behind, 0, 2).wait_recv()

    ends = low[...] + high[...]
    comb_a[0, :, 0] = even_a[0] - 0.5 * ends[:, 0:ya]
    comb_b[0, :, 0] = even_b[0] - 0.5 * (ends[:, ya : ya + yb] + ends[:, ya + yb : ya + 2 * yb])

    for pair in sent:
        for copy in pair:
            copy.wait_send()
    for copy in swaps:
        copy.wait_send()
    to_behind.wait_send()
    for e, d in enumerate(distances):
        @pl.when(lax.rem(me, 2 * d) == 0)
        def _(e=e, d=d):
            head_copy(low, behind, 1 + 2 * e, 1).wait_send()
            head_copy(high, behind, 2 + 2 * e, 2).wait_send()


def shards(n, grids_a, grids_b, coeffs):
    za, ya, nx = grids_a.shape[2:]
    zb, yb = grids_b.shape[2:4]
    finest = 2.0 * math.pi / max(nx, 2 * za * n)
    step, viscosity = 0.1 * finest, 0.2 * finest
    space_a = (2.0 * math.pi / (za * n), 2.0 * math.pi / ya, 2.0 * math.pi / nx)
    space_b = (2.0 * math.pi / (zb * n), 2.0 * math.pi / yb, 2.0 * math.pi / nx)
    consts = [jnp.asarray(m) for m in tables(za, ya, zb, yb, nx)]
    exponents = n.bit_length() - 1
    f32 = jnp.float32
    head_shape = (3, ya + 2 * yb, nx)
    vmem = pl.BlockSpec(memory_space=pltpu.VMEM)
    shape_a = jax.ShapeDtypeStruct(grids_a.shape, f32)
    shape_b = jax.ShapeDtypeStruct(grids_b.shape, f32)
    return pl.pallas_call(
        functools.partial(body, n, step, viscosity, space_a, space_b),
        out_shape=(shape_a, shape_b, shape_a, shape_b),
        in_specs=[pl.BlockSpec(memory_space=pltpu.SMEM)] + [vmem] * (2 + len(consts)),
        out_specs=(vmem,) * 4,
        scratch_shapes=[
            pltpu.VMEM((4, 3, za + 8, ya, nx), f32),
            pltpu.VMEM((4, 3, zb + 8, yb, nx), f32),
            pltpu.VMEM((3, za, ya, nx), f32),
            pltpu.VMEM((3, zb, yb, nx), f32),
            pltpu.VMEM((3, za, ya, nx), f32),
            pltpu.VMEM((3, zb, yb, nx), f32),
            pltpu.VMEM(head_shape, f32),
            pltpu.VMEM(head_shape, f32),
            pltpu.VMEM(head_shape, f32),
            pltpu.VMEM(head_shape, f32),
            pltpu.VMEM((3, zb, yb, nx), f32),
            pltpu.SemaphoreType.DMA((4, 2, 2)),
            pltpu.SemaphoreType.DMA((4, 2, 2)),
            pltpu.SemaphoreType.DMA((2,)),
            pltpu.SemaphoreType.DMA((2,)),
            pltpu.SemaphoreType.DMA((1 + 2 * exponents,)),
            pltpu.SemaphoreType.DMA((3,)),
        ],
        compiler_params=pltpu.CompilerParams(
            collective_id=0, has_side_effects=True, vmem_limit_bytes=32 * 2**20),
    )(coeffs, grids_a, grids_b, *consts)


def solution(mesh):
    split = P(("groups", "grid"), None, "slab", None, None)
    return jax.shard_map(
        functools.partial(shards, mesh.shape["slab"]),
        mesh=mesh,
        in_specs=(split, split, P()),
        out_specs=(split, split, split, split),
        check_vma=False,
    )
```

```python
import functools
import math

import jax
import jax.numpy as jnp
import ml_dtypes
import numpy as np
from jax import lax
from jax.experimental import pallas as pl
from jax.experimental.pallas import tpu as pltpu
from jax.sharding import PartitionSpec as P

first_coef = (0.8, -0.2, 4.0 / 105.0, -1.0 / 280.0)
second_coef = (1.6, -0.2, 8.0 / 315.0, -1.0 / 560.0)
second_mid = -205.0 / 72.0
MESH = pl.DeviceIdType.MESH


def hier_matrix(n):
    m = np.eye(n)
    for i in range(1, n):
        s = i & -i
        m[i, i - s] -= 0.5
        m[i, (i + s) % n] -= 0.5
    return m


def tables(za, ya, zb, yb, nx):
    hx, ha, hb = hier_matrix(nx), hier_matrix(ya), hier_matrix(yb)
    dx, da, db = (np.linalg.inv(h) for h in (hx, ha, hb))
    pa, pb = 3 * za, 3 * zb
    ratio = ya // yb
    spread_y = np.zeros((ya, yb))
    spread_y[np.arange(yb) * ratio, np.arange(yb)] = 1
    even = np.zeros((pa, pb))
    swap_a = np.zeros((pa, pa))
    swap_ab = np.zeros((pa, pb))
    swap_b = np.zeros((pb, pb))
    turned = (1, 0, 2)
    for c in range(3):
        for z in range(za):
            even[c * za + z, c * zb + 2 * z] = 1
            swap_a[c * za + z, turned[c] * za + z] = 1
            swap_ab[c * za + z, turned[c] * zb + 2 * z] = 1
        for z in range(zb):
            swap_b[c * zb + z, turned[c] * zb + z] = 1
    own_a = np.concatenate([np.kron(np.eye(pa), ha), np.kron(np.eye(pa), ha[::ratio])])
    own_b = np.concatenate([np.kron(even, spread_y @ hb), np.kron(np.eye(pb), hb)])
    pick_a, pick_b = hx[:: nx // ya], hx[:: nx // yb]
    other_a = np.concatenate([np.tile(pick_a, (pa, 1)), np.tile(pick_b, (pa, 1))])
    other_b = np.concatenate([np.tile(pick_a, (pa, 1)), np.tile(pick_b, (pb, 1))])
    mask_a = np.concatenate([np.kron(swap_a, np.ones((ya, ya))), np.kron(swap_a, np.ones((yb, ya)))])
    mask_b = np.concatenate([np.kron(swap_ab, np.ones((ya, yb))), np.kron(swap_b, np.ones((yb, yb)))])
    spread_a = np.zeros((ya, nx))
    spread_a[np.arange(ya), np.arange(ya) * (nx // ya)] = 1
    spread_b = np.zeros((yb, nx))
    spread_b[np.arange(yb), np.arange(yb) * (nx // yb)] = 1
    place_a = np.tile(ha.T @ spread_a, (pa, 1))
    place_b = np.tile(hb.T @ spread_b, (pb, 1))
    back_a = np.kron(np.eye(pa), da)
    back_b = np.kron(np.eye(pb), db)
    group = (hx.T, dx.T, own_a, own_b, other_a, other_b, mask_a, mask_b, place_a, place_b, back_a, back_b)
    return [np.asarray(m, dtype=ml_dtypes.bfloat16) for m in group]


def terms(x):
    hi = x.astype(jnp.bfloat16)
    lo = (x - hi.astype(jnp.float32)).astype(jnp.bfloat16)
    return hi, lo


def dot(a, b, contract):
    return lax.dot_general(a, b, (contract, ((), ())), preferred_element_type=jnp.float32)


def right(x, m):
    return sum(dot(t, m, ((1,), (0,))) for t in terms(x))


def left(m, x):
    return sum(dot(m, t, ((1,), (0,))) for t in terms(x))


def left_t(m, x):
    return sum(dot(m, t, ((1,), (1,))) for t in terms(x))


def body(n, step, viscosity, space_a, space_b, *refs):
    count = 12
    coeffs, a_ref, b_ref = refs[:3]
    tables_far = refs[3 : 3 + count]
    results = refs[3 + count : 7 + count]
    tables_near = refs[7 + count : 7 + 2 * count]
    (hx, dx, own_a, own_b, other_a, other_b, mask_a, mask_b,
     place_a, place_b, back_a, back_b) = tables_near
    (out_a, out_b, comb_a, comb_b, pad_a, pad_b, adv_a, adv_b, got_a, got_b, head, nxt, low, high, nodal,
     send_sem, recv_sem, swap_send, swap_recv, head_send, head_recv,
     in_sem, table_sem, out_sem) = refs[7 + 2 * count :]
    za, ya, nx = a_ref.shape[2:]
    zb, yb = b_ref.shape[2:4]
    rows = 3 * za * ya
    me = lax.axis_index("slab")
    member = lax.axis_index("grid")
    partner = 1 - member
    ahead, behind = lax.rem(me + 1, n), lax.rem(me + n - 1, n)

    distances = [2**e for e in range(n.bit_length() - 1)]
    offsets = sorted({o % n for d in distances for o in (d, n - d)})
    barrier = pltpu.get_barrier_semaphore()
    for o in offsets:
        pl.semaphore_signal(barrier, inc=1, device_id={"slab": lax.rem(me + o, n)}, device_id_type=MESH)
    pl.semaphore_signal(barrier, inc=1, device_id={"grid": partner}, device_id_type=MESH)
    loads = [
        pltpu.make_async_copy(a_ref.at[0], pad_a.at[0, :, pl.ds(4, za)], in_sem.at[0]),
        pltpu.make_async_copy(b_ref.at[0], pad_b.at[0, :, pl.ds(4, zb)], in_sem.at[1]),
    ]
    fetches = [
        pltpu.make_async_copy(far, near, table_sem.at[i])
        for i, (far, near) in enumerate(zip(tables_far, tables_near))
    ]
    for copy in loads + fetches:
        copy.start()
    stores = [
        pltpu.make_async_copy(near, far.at[0], out_sem.at[i])
        for i, (near, far) in enumerate(zip((out_a, out_b, comb_a, comb_b), results))
    ]
    for copy in loads:
        copy.wait()
    pl.semaphore_wait(barrier, len(offsets) + 1)

    def halo(pad, depth, stage, which):
        made = []
        for side, (first, target, peer) in enumerate(((depth, 0, ahead), (4, 4 + depth, behind))):
            made.append(pltpu.make_async_remote_copy(
                src_ref=pad.at[stage, :, pl.ds(first, 4)],
                dst_ref=pad.at[stage, :, pl.ds(target, 4)],
                send_sem=send_sem.at[stage, which, side],
                recv_sem=recv_sem.at[stage, which, side],
                device_id={"slab": peer}, device_id_type=MESH))
        for copy in made:
            copy.start()
        return made

    def flat_rate(f, spaces):
        planes, y, x = f.shape[1:]
        rows_f = f.reshape(3 * planes * y, x)
        blocks = f.reshape(3 * planes, y, x)
        mid = second_mid * viscosity * sum(1.0 / (h * h) for h in spaces)

        def direction(value, axis, h):
            grad = curv = None
            length = value.shape[axis]
            for k in range(1, 5):
                fwd = pltpu.roll(value, length - k, axis)
                bwd = pltpu.roll(value, k, axis)
                g = (first_coef[k - 1] / h) * (fwd - bwd)
                c = (viscosity * second_coef[k - 1] / (h * h)) * (fwd + bwd)
                grad = g if grad is None else grad + g
                curv = c if curv is None else curv + c
            return grad.reshape(f.shape), curv.reshape(f.shape)

        xg, xc = direction(rows_f, 1, spaces[2])
        yg, yc = direction(blocks, 1, spaces[1])
        return mid * f + xc + yc - (f[0:1] * xg + f[1:2] * yg)

    def z_rate(pad, stage, depth, h):
        f = pad[stage, :, 4 : 4 + depth]
        grad = curv = None
        for k in range(1, 5):
            fwd = pad[stage, :, 4 + k : 4 + k + depth]
            bwd = pad[stage, :, 4 - k : 4 - k + depth]
            g = (first_coef[k - 1] / h) * (fwd - bwd)
            c = (viscosity * second_coef[k - 1] / (h * h)) * (fwd + bwd)
            grad = g if grad is None else grad + g
            curv = c if curv is None else curv + c
        return curv - f[2:3] * grad

    grids = ((pad_a, za, space_a, adv_a), (pad_b, zb, space_b, adv_b))
    swaps = []
    flights = [halo(pad, depth, 0, w) for w, (pad, depth, _, _) in enumerate(grids)]
    sent = list(flights)
    for stage in range(4):
        flat = [flat_rate(pad[stage, :, 4 : 4 + depth], spaces) for pad, depth, spaces, _ in grids]
        coming = []
        for w, (pad, depth, spaces, adv) in enumerate(grids):
            for copy in flights[w]:
                copy.wait_recv()
            k = flat[w] + z_rate(pad, stage, depth, spaces[0])
            base = pad[0, :, 4 : 4 + depth]
            share = step / 6.0 * (1.0, 2.0, 2.0, 1.0)[stage]
            adv[...] = (base if stage == 0 else adv[...]) + share * k
            if stage < 3:
                pad[stage + 1, :, 4 : 4 + depth] = base + (0.5, 0.5, 1.0)[stage] * step * k
                coming.append(halo(pad, depth, stage + 1, w))
            else:
                copy = pltpu.make_async_remote_copy(
                    src_ref=adv, dst_ref=(got_a, got_b)[w],
                    send_sem=swap_send.at[w], recv_sem=swap_recv.at[w],
                    device_id={"grid": partner}, device_id_type=MESH)
                copy.start()
                swaps.append(copy)
        if stage < 3:
            flights = coming
            sent.extend(coming)

    for copy in fetches:
        copy.wait()
    weight = [coeffs[i].astype(jnp.float32) for i in (member, partner, 2 + member, 2 + partner)]
    mine_a = weight[0] * left(own_a[...], right(adv_a[...].reshape(rows, nx), hx[...]))
    mine_b = weight[2] * left(own_b[...], right(adv_b[...].reshape(rows, nx), hx[...]))

    def other(got, pick, mask, place):
        crossed = left_t(pick[...], got[...].reshape(rows, nx)) * mask[...].astype(jnp.float32)
        return right(crossed, place[...])

    swaps[0].wait_recv()
    sum_a = mine_a + weight[1] * other(got_a, other_a, mask_a, place_a)
    swaps[1].wait_recv()
    sum_b = mine_b + weight[3] * other(got_b, other_b, mask_b, place_b)
    nodal_a = sum_a[:rows] + sum_b[:rows]
    level_a = nodal_a.reshape(3, za, ya, nx)
    part_q = sum_a[rows:].reshape(3, za, yb, nx)
    part_p = sum_b[rows:].reshape(3, zb, yb, nx)

    coarse = head.at[:, pl.ds(0, ya + yb)]
    head[:, 0:ya] = level_a[:, 0]
    head[:, ya : ya + yb] = part_p[:, 0] + part_q[:, 0]
    head[:, ya + yb : ya + 2 * yb] = part_q[:, 0]

    @pl.when(me == 0)
    def _():
        low[...] = jnp.zeros_like(low)

    @pl.when(me == 0)
    def _():
        high[...] = jnp.zeros_like(high)

    def head_copy(target, peer, send, recv):
        return pltpu.make_async_remote_copy(
            src_ref=head if recv == 0 else coarse, dst_ref=target, send_sem=head_send.at[send], recv_sem=head_recv.at[recv],
            device_id={"slab": peer}, device_id_type=MESH)

    to_behind = head_copy(nxt, behind, 0, 0)
    to_behind.start()
    for e, d in enumerate(distances):
        @pl.when(lax.rem(me, 2 * d) == 0)
        def _(e=e, d=d):
            head_copy(low, lax.rem(me + d, n), 1 + 2 * e, 1).start()
            if 1 < d < n // 2:
                head_copy(high, lax.rem(me + n - d, n), 2 + 2 * e, 2).start()

    out_a[...] = left(back_a[...], right(nodal_a, dx[...])).reshape(3, za, ya, nx)
    stores[0].start()

    to_behind.wait_recv()
    next_a = nxt[:, 0:ya]
    next_b = nxt[:, ya : ya + yb]
    next_q = nxt[:, ya + yb : ya + 2 * yb]
    next_p = next_b - next_q
    for z in range(za):
        q_now = part_q[:, z]
        q_next = part_q[:, z + 1] if z + 1 < za else next_q
        p_next = part_p[:, 2 * z + 2] if z + 1 < za else next_p
        nodal[:, 2 * z] = part_p[:, 2 * z] + q_now
        nodal[:, 2 * z + 1] = part_p[:, 2 * z + 1] + 0.5 * (q_now + q_next)
        comb_b[:, 2 * z + 1] = part_p[:, 2 * z + 1] - 0.5 * (part_p[:, 2 * z] + p_next)
    out_b[...] = left(back_b[...], right(nodal[...].reshape(rows, nx), dx[...])).reshape(3, zb, yb, nx)
    stores[1].start()

    even_b = [part_p[:, 2 * z] + part_q[:, z] for z in range(za)] + [next_b]
    even_a = [level_a[:, z] for z in range(za)] + [next_a]
    for z in range(1, za):
        s = z & -z
        comb_a[:, z] = even_a[z] - 0.5 * (even_a[z - s] + even_a[z + s])
        comb_b[:, 2 * z] = even_b[z] - 0.5 * (even_b[z - s] + even_b[z + s])

    @pl.when(me != 0)
    def _():
        head_copy(low, behind, 0, 1).wait_recv()

    @pl.when((me != 0) & (lax.rem(me, 2) == 0) & (me != n // 2))
    def _():
        head_copy(high, behind, 0, 2).wait_recv()

    @pl.when(lax.rem(me, 2) == 1)
    def _():
        high[...] = nxt[:, 0 : ya + yb]

    @pl.when(me == n // 2)
    def _():
        high[...] = low[...]

    ends = low[...] + high[...]
    comb_a[:, 0] = even_a[0] - 0.5 * ends[:, 0:ya]
    comb_b[:, 0] = even_b[0] - 0.5 * ends[:, ya : ya + yb]
    stores[2].start()
    stores[3].start()

    for pair in sent:
        for copy in pair:
            copy.wait_send()
    for copy in swaps:
        copy.wait_send()
    to_behind.wait_send()
    for e, d in enumerate(distances):
        @pl.when(lax.rem(me, 2 * d) == 0)
        def _(e=e, d=d):
            head_copy(low, behind, 1 + 2 * e, 1).wait_send()
            if 1 < d < n // 2:
                head_copy(high, behind, 2 + 2 * e, 2).wait_send()
    for copy in stores:
        copy.wait()


def shards(n, grids_a, grids_b, coeffs):
    za, ya, nx = grids_a.shape[2:]
    zb, yb = grids_b.shape[2:4]
    finest = 2.0 * math.pi / max(nx, 2 * za * n)
    step, viscosity = 0.1 * finest, 0.2 * finest
    space_a = (2.0 * math.pi / (za * n), 2.0 * math.pi / ya, 2.0 * math.pi / nx)
    space_b = (2.0 * math.pi / (zb * n), 2.0 * math.pi / yb, 2.0 * math.pi / nx)
    consts = [jnp.asarray(m) for m in tables(za, ya, zb, yb, nx)]
    exponents = n.bit_length() - 1
    f32 = jnp.float32
    head_shape = (3, ya + 2 * yb, nx)
    coarse_shape = (3, ya + yb, nx)
    far = pl.BlockSpec(memory_space=pltpu.HBM)
    shape_a = jax.ShapeDtypeStruct(grids_a.shape, f32)
    shape_b = jax.ShapeDtypeStruct(grids_b.shape, f32)
    return pl.pallas_call(
        functools.partial(body, n, step, viscosity, space_a, space_b),
        out_shape=(shape_a, shape_b, shape_a, shape_b),
        in_specs=[pl.BlockSpec(memory_space=pltpu.SMEM)] + [far] * (2 + len(consts)),
        out_specs=(far,) * 4,
        scratch_shapes=[pltpu.VMEM(m.shape, m.dtype) for m in consts] + [
            pltpu.VMEM((3, za, ya, nx), f32),
            pltpu.VMEM((3, zb, yb, nx), f32),
            pltpu.VMEM((3, za, ya, nx), f32),
            pltpu.VMEM((3, zb, yb, nx), f32),
            pltpu.VMEM((4, 3, za + 8, ya, nx), f32),
            pltpu.VMEM((4, 3, zb + 8, yb, nx), f32),
            pltpu.VMEM((3, za, ya, nx), f32),
            pltpu.VMEM((3, zb, yb, nx), f32),
            pltpu.VMEM((3, za, ya, nx), f32),
            pltpu.VMEM((3, zb, yb, nx), f32),
            pltpu.VMEM(head_shape, f32),
            pltpu.VMEM(head_shape, f32),
            pltpu.VMEM(coarse_shape, f32),
            pltpu.VMEM(coarse_shape, f32),
            pltpu.VMEM((3, zb, yb, nx), f32),
            pltpu.SemaphoreType.DMA((4, 2, 2)),
            pltpu.SemaphoreType.DMA((4, 2, 2)),
            pltpu.SemaphoreType.DMA((2,)),
            pltpu.SemaphoreType.DMA((2,)),
            pltpu.SemaphoreType.DMA((1 + 2 * exponents,)),
            pltpu.SemaphoreType.DMA((3,)),
            pltpu.SemaphoreType.DMA((2,)),
            pltpu.SemaphoreType.DMA((12,)),
            pltpu.SemaphoreType.DMA((4,)),
        ],
        compiler_params=pltpu.CompilerParams(
            collective_id=0, has_side_effects=True, vmem_limit_bytes=62 * 2**20),
    )(coeffs, grids_a, grids_b, *consts)


def solution(mesh):
    split = P(("groups", "grid"), None, "slab", None, None)
    return jax.shard_map(
        functools.partial(shards, mesh.shape["slab"]),
        mesh=mesh,
        in_specs=(split, split, P()),
        out_specs=(split, split, split, split),
        check_vma=False,
    )
```

```python
import functools
import math

import jax
import jax.numpy as jnp
import ml_dtypes
import numpy as np
from jax import lax
from jax.experimental import pallas as pl
from jax.experimental.pallas import tpu as pltpu
from jax.sharding import PartitionSpec as P

first_coef = (0.8, -0.2, 4.0 / 105.0, -1.0 / 280.0)
second_coef = (1.6, -0.2, 8.0 / 315.0, -1.0 / 560.0)
second_mid = -205.0 / 72.0
MESH = pl.DeviceIdType.MESH


def hier_matrix(n):
    m = np.eye(n)
    for i in range(1, n):
        s = i & -i
        m[i, i - s] -= 0.5
        m[i, (i + s) % n] -= 0.5
    return m


def tables(za, ya, zb, yb, nx):
    hx, ha, hb = hier_matrix(nx), hier_matrix(ya), hier_matrix(yb)
    dx, da, db = (np.linalg.inv(h) for h in (hx, ha, hb))
    pa, pb = 3 * za, 3 * zb
    ratio = ya // yb
    spread_y = np.zeros((ya, yb))
    spread_y[np.arange(yb) * ratio, np.arange(yb)] = 1
    even = np.zeros((pa, pb))
    swap_a = np.zeros((pa, pa))
    swap_ab = np.zeros((pa, pb))
    swap_b = np.zeros((pb, pb))
    turned = (1, 0, 2)
    for c in range(3):
        for z in range(za):
            even[c * za + z, c * zb + 2 * z] = 1
            swap_a[c * za + z, turned[c] * za + z] = 1
            swap_ab[c * za + z, turned[c] * zb + 2 * z] = 1
        for z in range(zb):
            swap_b[c * zb + z, turned[c] * zb + z] = 1
    own_a = np.concatenate([np.kron(np.eye(pa), ha), np.kron(np.eye(pa), ha[::ratio])])
    own_b = np.concatenate([np.kron(even, spread_y @ hb), np.kron(np.eye(pb), hb)])
    pick_a, pick_b = hx[:: nx // ya], hx[:: nx // yb]
    other_a = np.concatenate([np.tile(pick_a, (pa, 1)), np.tile(pick_b, (pa, 1))])
    other_b = np.concatenate([np.tile(pick_a, (pa, 1)), np.tile(pick_b, (pb, 1))])
    mask_a = np.concatenate([np.kron(swap_a, np.ones((ya, ya))), np.kron(swap_a, np.ones((yb, ya)))])
    mask_b = np.concatenate([np.kron(swap_ab, np.ones((ya, yb))), np.kron(swap_b, np.ones((yb, yb)))])
    spread_a = np.zeros((ya, nx))
    spread_a[np.arange(ya), np.arange(ya) * (nx // ya)] = 1
    spread_b = np.zeros((yb, nx))
    spread_b[np.arange(yb), np.arange(yb) * (nx // yb)] = 1
    place_a = np.tile(ha.T @ spread_a, (pa, 1))
    place_b = np.tile(hb.T @ spread_b, (pb, 1))
    back_a = np.kron(np.eye(pa), da)
    back_b = np.kron(np.eye(pb), db)
    group = (hx.T, dx.T, own_a, own_b, other_a, other_b, mask_a, mask_b, place_a, place_b, back_a, back_b)
    return [np.asarray(m, dtype=ml_dtypes.bfloat16) for m in group]


def terms(x):
    hi = x.astype(jnp.bfloat16)
    lo = (x - hi.astype(jnp.float32)).astype(jnp.bfloat16)
    return hi, lo


def dot(a, b, contract):
    return lax.dot_general(a, b, (contract, ((), ())), preferred_element_type=jnp.float32)


def right(x, m):
    return sum(dot(t, m, ((1,), (0,))) for t in terms(x))


def left(m, x):
    return sum(dot(m, t, ((1,), (0,))) for t in terms(x))


def left_t(m, x):
    return sum(dot(m, t, ((1,), (1,))) for t in terms(x))


def body(n, step, viscosity, space_a, space_b, *refs):
    count = 12
    coeffs, a_ref, b_ref = refs[:3]
    tables_far = refs[3 : 3 + count]
    results = refs[3 + count : 7 + count]
    tables_near = refs[7 + count : 7 + 2 * count]
    (hx, dx, own_a, own_b, other_a, other_b, mask_a, mask_b,
     place_a, place_b, back_a, back_b) = tables_near
    (out_a, out_b, comb_a, comb_b, pad_a, pad_b, adv_a, adv_b, got_a, got_b, head, nxt, low, high, nodal,
     send_sem, recv_sem, swap_send, swap_recv, head_send, head_recv,
     in_sem, table_sem, out_sem) = refs[7 + 2 * count :]
    za, ya, nx = a_ref.shape[2:]
    zb, yb = b_ref.shape[2:4]
    rows = 3 * za * ya
    me = lax.axis_index("slab")
    member = lax.axis_index("grid")
    partner = 1 - member
    ahead, behind = lax.rem(me + 1, n), lax.rem(me + n - 1, n)

    distances = [2**e for e in range(n.bit_length() - 1)]
    offsets = sorted({o % n for d in distances for o in (d, n - d)})
    barrier = pltpu.get_barrier_semaphore()
    for o in offsets:
        pl.semaphore_signal(barrier, inc=1, device_id={"slab": lax.rem(me + o, n)}, device_id_type=MESH)
    pl.semaphore_signal(barrier, inc=1, device_id={"grid": partner}, device_id_type=MESH)
    loads = [
        pltpu.make_async_copy(a_ref.at[0], pad_a.at[0, :, pl.ds(4, za)], in_sem.at[0]),
        pltpu.make_async_copy(b_ref.at[0], pad_b.at[0, :, pl.ds(4, zb)], in_sem.at[1]),
    ]
    fetches = [
        pltpu.make_async_copy(far, near, table_sem.at[i])
        for i, (far, near) in enumerate(zip(tables_far, tables_near))
    ]
    for copy in loads + fetches:
        copy.start()
    stores = [
        pltpu.make_async_copy(near, far.at[0], out_sem.at[i])
        for i, (near, far) in enumerate(zip((out_a, out_b, comb_a, comb_b), results))
    ]
    for copy in loads:
        copy.wait()
    pl.semaphore_wait(barrier, len(offsets) + 1)

    def halo(pad, depth, stage, which):
        made = []
        for side, (first, target, peer) in enumerate(((depth, 0, ahead), (4, 4 + depth, behind))):
            made.append(pltpu.make_async_remote_copy(
                src_ref=pad.at[stage, :, pl.ds(first, 4)],
                dst_ref=pad.at[stage, :, pl.ds(target, 4)],
                send_sem=send_sem.at[stage, which, side],
                recv_sem=recv_sem.at[stage, which, side],
                device_id={"slab": peer}, device_id_type=MESH))
        for copy in made:
            copy.start()
        return made

    def flat_rate(f, spaces):
        planes, y, x = f.shape[1:]
        rows_f = f.reshape(3 * planes * y, x)
        blocks = f.reshape(3 * planes, y, x)
        mid = second_mid * viscosity * sum(1.0 / (h * h) for h in spaces)

        def direction(value, axis, h):
            grad = curv = None
            length = value.shape[axis]
            for k in range(1, 5):
                fwd = pltpu.roll(value, length - k, axis)
                bwd = pltpu.roll(value, k, axis)
                g = (first_coef[k - 1] / h) * (fwd - bwd)
                c = (viscosity * second_coef[k - 1] / (h * h)) * (fwd + bwd)
                grad = g if grad is None else grad + g
                curv = c if curv is None else curv + c
            return grad.reshape(f.shape), curv.reshape(f.shape)

        xg, xc = direction(rows_f, 1, spaces[2])
        yg, yc = direction(blocks, 1, spaces[1])
        return mid * f + xc + yc - (f[0:1] * xg + f[1:2] * yg)

    def z_rate(pad, stage, depth, h):
        f = pad[stage, :, 4 : 4 + depth]
        grad = curv = None
        for k in range(1, 5):
            fwd = pad[stage, :, 4 + k : 4 + k + depth]
            bwd = pad[stage, :, 4 - k : 4 - k + depth]
            g = (first_coef[k - 1] / h) * (fwd - bwd)
            c = (viscosity * second_coef[k - 1] / (h * h)) * (fwd + bwd)
            grad = g if grad is None else grad + g
            curv = c if curv is None else curv + c
        return curv - f[2:3] * grad

    grids = ((pad_a, za, space_a, adv_a), (pad_b, zb, space_b, adv_b))
    swaps = []
    flights = [halo(pad, depth, 0, w) for w, (pad, depth, _, _) in enumerate(grids)]
    sent = list(flights)
    for stage in range(4):
        flat = [flat_rate(pad[stage, :, 4 : 4 + depth], spaces) for pad, depth, spaces, _ in grids]
        coming = []
        for w, (pad, depth, spaces, adv) in enumerate(grids):
            for copy in flights[w]:
                copy.wait_recv()
            k = flat[w] + z_rate(pad, stage, depth, spaces[0])
            base = pad[0, :, 4 : 4 + depth]
            share = step / 6.0 * (1.0, 2.0, 2.0, 1.0)[stage]
            adv[...] = (base if stage == 0 else adv[...]) + share * k
            if stage < 3:
                pad[stage + 1, :, 4 : 4 + depth] = base + (0.5, 0.5, 1.0)[stage] * step * k
                coming.append(halo(pad, depth, stage + 1, w))
            else:
                copy = pltpu.make_async_remote_copy(
                    src_ref=adv, dst_ref=(got_a, got_b)[w],
                    send_sem=swap_send.at[w], recv_sem=swap_recv.at[w],
                    device_id={"grid": partner}, device_id_type=MESH)
                copy.start()
                swaps.append(copy)
        if stage < 3:
            flights = coming
            sent.extend(coming)

    for copy in fetches:
        copy.wait()
    weight = [coeffs[i].astype(jnp.float32) for i in (member, partner, 2 + member, 2 + partner)]
    mine_a = weight[0] * left(own_a[...], right(adv_a[...].reshape(rows, nx), hx[...]))
    mine_b = weight[2] * left(own_b[...], right(adv_b[...].reshape(rows, nx), hx[...]))

    def other(got, pick, mask, place):
        crossed = left_t(pick[...], got[...].reshape(rows, nx)) * mask[...].astype(jnp.float32)
        return right(crossed, place[...])

    swaps[0].wait_recv()
    sum_a = mine_a + weight[1] * other(got_a, other_a, mask_a, place_a)
    swaps[1].wait_recv()
    sum_b = mine_b + weight[3] * other(got_b, other_b, mask_b, place_b)
    nodal_a = sum_a[:rows] + sum_b[:rows]
    level_a = nodal_a.reshape(3, za, ya, nx)
    part_q = sum_a[rows:].reshape(3, za, yb, nx)
    part_p = sum_b[rows:].reshape(3, zb, yb, nx)

    coarse = head.at[:, pl.ds(0, ya + yb)]
    head[:, 0:ya] = level_a[:, 0]
    head[:, ya : ya + yb] = part_p[:, 0] + part_q[:, 0]
    head[:, ya + yb : ya + 2 * yb] = part_q[:, 0]

    @pl.when(me == 0)
    def _():
        low[...] = jnp.zeros_like(low)

    @pl.when(me == 0)
    def _():
        high[...] = jnp.zeros_like(high)

    def head_copy(target, peer, send, recv):
        return pltpu.make_async_remote_copy(
            src_ref=head if recv == 0 else coarse, dst_ref=target, send_sem=head_send.at[send], recv_sem=head_recv.at[recv],
            device_id={"slab": peer}, device_id_type=MESH)

    to_behind = head_copy(nxt, behind, 0, 0)
    to_behind.start()
    for e, d in enumerate(distances):
        @pl.when(lax.rem(me, 2 * d) == 0)
        def _(e=e, d=d):
            head_copy(low, lax.rem(me + d, n), 1 + 2 * e, 1).start()
            if 1 < d < n // 2:
                head_copy(high, lax.rem(me + n - d, n), 2 + 2 * e, 2).start()

    out_a[...] = left(back_a[...], right(nodal_a, dx[...])).reshape(3, za, ya, nx)
    stores[0].start()

    to_behind.wait_recv()
    next_a = nxt[:, 0:ya]
    next_b = nxt[:, ya : ya + yb]
    next_q = nxt[:, ya + yb : ya + 2 * yb]
    next_p = next_b - next_q
    for z in range(za):
        q_now = part_q[:, z]
        q_next = part_q[:, z + 1] if z + 1 < za else next_q
        p_next = part_p[:, 2 * z + 2] if z + 1 < za else next_p
        nodal[:, 2 * z] = part_p[:, 2 * z] + q_now
        nodal[:, 2 * z + 1] = part_p[:, 2 * z + 1] + 0.5 * (q_now + q_next)
        comb_b[:, 2 * z + 1] = part_p[:, 2 * z + 1] - 0.5 * (part_p[:, 2 * z] + p_next)
    out_b[...] = left(back_b[...], right(nodal[...].reshape(rows, nx), dx[...])).reshape(3, zb, yb, nx)
    stores[1].start()

    even_b = [part_p[:, 2 * z] + part_q[:, z] for z in range(za)] + [next_b]
    even_a = [level_a[:, z] for z in range(za)] + [next_a]
    for z in range(1, za):
        s = z & -z
        comb_a[:, z] = even_a[z] - 0.5 * (even_a[z - s] + even_a[z + s])
        comb_b[:, 2 * z] = even_b[z] - 0.5 * (even_b[z - s] + even_b[z + s])

    @pl.when(me != 0)
    def _():
        head_copy(low, behind, 0, 1).wait_recv()

    @pl.when((me != 0) & (lax.rem(me, 2) == 0) & (me != n // 2))
    def _():
        head_copy(high, behind, 0, 2).wait_recv()

    @pl.when(lax.rem(me, 2) == 1)
    def _():
        high[...] = nxt[:, 0 : ya + yb]

    @pl.when(me == n // 2)
    def _():
        high[...] = low[...]

    ends = low[...] + high[...]
    comb_a[:, 0] = even_a[0] - 0.5 * ends[:, 0:ya]
    comb_b[:, 0] = even_b[0] - 0.5 * ends[:, ya : ya + yb]
    stores[2].start()
    stores[3].start()

    for pair in sent:
        for copy in pair:
            copy.wait_send()
    for copy in swaps:
        copy.wait_send()
    to_behind.wait_send()
    for e, d in enumerate(distances):
        @pl.when(lax.rem(me, 2 * d) == 0)
        def _(e=e, d=d):
            head_copy(low, behind, 1 + 2 * e, 1).wait_send()
            if 1 < d < n // 2:
                head_copy(high, behind, 2 + 2 * e, 2).wait_send()
    for copy in stores:
        copy.wait()


def hand_over(*refs):
    count = 4
    source, target, held, sems = refs[:count], refs[count : 2 * count], refs[2 * count : 3 * count], refs[3 * count]
    loads = [pltpu.make_async_copy(source[i], held[i], sems.at[0, i]) for i in range(count)]
    stores = [pltpu.make_async_copy(held[i], target[i], sems.at[1, i]) for i in range(count)]
    for copy in loads:
        copy.start()
    for load, store in zip(loads, stores):
        load.wait()
        store.start()
    for copy in stores:
        copy.wait()


def shards(n, grids_a, grids_b, coeffs):
    za, ya, nx = grids_a.shape[2:]
    zb, yb = grids_b.shape[2:4]
    finest = 2.0 * math.pi / max(nx, 2 * za * n)
    step, viscosity = 0.1 * finest, 0.2 * finest
    space_a = (2.0 * math.pi / (za * n), 2.0 * math.pi / ya, 2.0 * math.pi / nx)
    space_b = (2.0 * math.pi / (zb * n), 2.0 * math.pi / yb, 2.0 * math.pi / nx)
    consts = [jnp.asarray(m) for m in tables(za, ya, zb, yb, nx)]
    exponents = n.bit_length() - 1
    f32 = jnp.float32
    head_shape = (3, ya + 2 * yb, nx)
    coarse_shape = (3, ya + yb, nx)
    far = pl.BlockSpec(memory_space=pltpu.HBM)
    shape_a = jax.ShapeDtypeStruct(grids_a.shape, f32)
    shape_b = jax.ShapeDtypeStruct(grids_b.shape, f32)
    results = pl.pallas_call(
        functools.partial(body, n, step, viscosity, space_a, space_b),
        out_shape=(shape_a, shape_b, shape_a, shape_b),
        in_specs=[pl.BlockSpec(memory_space=pltpu.SMEM)] + [far] * (2 + len(consts)),
        out_specs=(far,) * 4,
        scratch_shapes=[pltpu.VMEM(m.shape, m.dtype) for m in consts] + [
            pltpu.VMEM((3, za, ya, nx), f32),
            pltpu.VMEM((3, zb, yb, nx), f32),
            pltpu.VMEM((3, za, ya, nx), f32),
            pltpu.VMEM((3, zb, yb, nx), f32),
            pltpu.VMEM((4, 3, za + 8, ya, nx), f32),
            pltpu.VMEM((4, 3, zb + 8, yb, nx), f32),
            pltpu.VMEM((3, za, ya, nx), f32),
            pltpu.VMEM((3, zb, yb, nx), f32),
            pltpu.VMEM((3, za, ya, nx), f32),
            pltpu.VMEM((3, zb, yb, nx), f32),
            pltpu.VMEM(head_shape, f32),
            pltpu.VMEM(head_shape, f32),
            pltpu.VMEM(coarse_shape, f32),
            pltpu.VMEM(coarse_shape, f32),
            pltpu.VMEM((3, zb, yb, nx), f32),
            pltpu.SemaphoreType.DMA((4, 2, 2)),
            pltpu.SemaphoreType.DMA((4, 2, 2)),
            pltpu.SemaphoreType.DMA((2,)),
            pltpu.SemaphoreType.DMA((2,)),
            pltpu.SemaphoreType.DMA((1 + 2 * exponents,)),
            pltpu.SemaphoreType.DMA((3,)),
            pltpu.SemaphoreType.DMA((2,)),
            pltpu.SemaphoreType.DMA((12,)),
            pltpu.SemaphoreType.DMA((4,)),
        ],
        compiler_params=pltpu.CompilerParams(
            collective_id=0, has_side_effects=True, vmem_limit_bytes=62 * 2**20),
    )(coeffs, grids_a, grids_b, *consts)
    return pl.pallas_call(
        hand_over,
        out_shape=(shape_a, shape_b, shape_a, shape_b),
        in_specs=[far] * 4,
        out_specs=(far,) * 4,
        scratch_shapes=[pltpu.VMEM(r.shape, f32) for r in results] + [pltpu.SemaphoreType.DMA((2, 4))],
        compiler_params=pltpu.CompilerParams(vmem_limit_bytes=62 * 2**20),
    )(*results)


def solution(mesh):
    split = P(("groups", "grid"), None, "slab", None, None)
    return jax.shard_map(
        functools.partial(shards, mesh.shape["slab"]),
        mesh=mesh,
        in_specs=(split, split, P()),
        out_specs=(split, split, split, split),
        check_vma=False,
    )
```
